32 devices in a mesh: groups: 2 (over x), cell: 16 (over z, y, core).
Axes of the slice: x: 2, y: 2, z: 4, core: 2. Of those that a mesh axis runs over, the one named last changes fastest.
Arguments:
- features: bfloat16 [256, 512, 128], P(('groups', 'cell')), parts along dimension 0, may hold values from -6 to 6
- neighbour_table: int32 [256, 26], P(('groups', 'cell')), parts along dimension 0, may hold values from 0 to 24
- send_lists: int32 [32, 4, 4], P(('groups', 'cell')), parts along dimension 0, may hold values from 0 to 7
- coarse_target: int32 [256], P('groups'), parts along dimension 0, may hold values from 0 to 31, as said below
- conv_weight: bfloat16 [3456, 128], replicated, may hold values from -0.109375 to 0.109375
- norm_gain: float32 [128], replicated, may hold values from 0.1 to 1.9
- norm_shift: float32 [128], replicated, may hold values from -3 to 3
- reduce_weight_matrix: bfloat16 [1024, 128], replicated, may hold values from -0.25 to 0.25
Outputs:
- fine_output_features: bfloat16 [256, 512, 128], P(('groups', 'cell')), parts along dimension 0
- coarse_out: bfloat16 [64, 512, 128], P(('groups', 'cell')), parts along dimension 0
The draws below stay inside these ranges and needn't reach their ends.
There are 2 independent parts, one for each index of `groups`. The reference program is written for one: setup_inputs(seed, part) draws one part's arguments, and reference() takes and returns one part's arrays. A program takes and returns all parts, laid end to end along the dimension named above; an argument that names none is the same for every part. Nothing has to cross between parts.
Inputs may be any that keep to these rules, and one draw needn't show every extreme that they name: `neighbour_table`: the value 8 + 4 * 4 marks an empty neighbour; smaller values are local blocks, then halo slots. `coarse_target`: within each pair of devices 2m and 2m + 1 the values of their 16 blocks are distinct.
All inputs are finite; a program needn't handle non-finite values.
Results may differ from the reference program's by a relative error of at most 0.005.
Values may be sent and summed in bfloat16 or wider, within the bound.
A program may use at most 64 MiB of HBM per device.

```python
import jax
import jax.numpy as jnp
from jax import lax

CH = 128
VOX = 512
B_DEV = 8
NOFF = 4
HCAP = 4
C_DEV = 2
NBLK = 128
N_CELL = 16


def draw_coarse_target(key, part):
    pair_keys = jax.random.split(key, N_CELL // 2)

    def one_pair(pair_key):
        first_key, second_key = jax.random.split(pair_key)
        middle = jax.random.permutation(first_key, 16 * C_DEV - 2)[:2 * B_DEV - 2] + 1
        ends = jnp.array([0, 16 * C_DEV - 1], dtype=jnp.int32)
        values = jnp.concatenate([ends, middle.astype(jnp.int32)], axis=0)
        order = jax.random.permutation(second_key, 2 * B_DEV)
        return values[order]
    return jax.vmap(one_pair)(pair_keys).reshape(-1).astype(jnp.int32)


def touch_ends(values, rng, low, high):
    place = [jax.random.randint(jax.random.fold_in(rng, axis), (), 0, length) for axis, length in enumerate(values.shape)]
    main_axis = values.shape.index(max(values.shape))
    beside = place[:main_axis] + [(place[main_axis] + 1) % values.shape[main_axis]] + place[main_axis + 1:]
    return values.at[tuple(place)].set(low).at[tuple(beside)].set(high)


def shard_levels(key, dims, shards, least, top_value):
    level, own = 1.0, jax.random.fold_in(key, 6)
    for position, shards_of in shards:
        draws = jnp.exp(jax.random.uniform(jax.random.fold_in(own, position), (shards_of,), jnp.float32, least / len(shards), top_value / len(shards)))
        level = level * jnp.repeat(draws, dims[position] // shards_of).reshape([-1 if axis == position else 1 for axis in range(len(dims))])
    return level


def gaussian(rng, dims, spread, reach, shards=(), kind=jnp.bfloat16):
    factor_of = shard_levels(rng, dims, shards, -0.22, 0.18) if shards else 1.0
    values = jax.random.normal(rng, dims, jnp.float32) * spread * factor_of
    return jnp.minimum(jnp.maximum(values, -reach), reach).astype(kind)


def setup_inputs(seed: int = 0, part: int = 0) -> dict:
    keys = jax.random.split(jax.random.key(seed), 9)
    part_splits = jax.random.split(jax.random.fold_in(keys[8], part), 9)
    features = gaussian(part_splits[0], (NBLK, VOX, CH), 1.0, 6.0, ((0, 16),))
    neighbour_table = touch_ends(jax.random.randint(part_splits[1], (NBLK, 26), 0, B_DEV + NOFF * HCAP + 1), jax.random.fold_in(part_splits[1], 1), 0, B_DEV + NOFF * HCAP).astype(jnp.int32)
    send_lists = touch_ends(jax.random.randint(part_splits[2], (N_CELL, NOFF, HCAP), 0, B_DEV), jax.random.fold_in(part_splits[2], 1), 0, B_DEV - 1).astype(jnp.int32)
    coarse_target = draw_coarse_target(jax.random.fold_in(jax.random.fold_in(keys[8], part), 71), part)
    conv_weight = gaussian(keys[4], (27 * CH, CH), (27 * CH) ** -0.5, 0.109375)
    norm_gain = jnp.clip(1.0 + 0.18 * jax.random.normal(keys[5], (CH,), jnp.float32), 0.1, 1.9)
    norm_shift = gaussian(keys[6], (CH,), 0.5, 3.0, (), jnp.float32)
    reduce_weight_matrix = gaussian(keys[7], (8 * CH, CH), (4 * CH) ** -0.5, 0.25)
    return {"features": features, "neighbour_table": neighbour_table, "send_lists": send_lists, "coarse_target": coarse_target, "conv_weight": conv_weight, "norm_gain": norm_gain, "norm_shift": norm_shift, "reduce_weight_matrix": reduce_weight_matrix}


OFFSETS = (1, -1, 2, -2)


def take_slab(block, offset, device_dimension):
    if offset == -1:
        return lax.slice_in_dim(block, 7, 8, axis=device_dimension)
    if offset == 1:
        return lax.slice_in_dim(block, 0, 1, axis=device_dimension)
    return block


def conv_block(stacked, conv_weight, channel_total):
    blocks = stacked.reshape(27, 8, 8, 8, channel_total)
    planes = []
    for shift_x in (-1, 0, 1):
        rows_list = []
        for shift_y in (-1, 0, 1):
            cols_list = []
            for shift_z in (-1, 0, 1):
                number = (shift_x + 1) * 9 + (shift_y + 1) * 3 + (shift_z + 1)
                piece = take_slab(blocks[number], shift_x, 0)
                piece = take_slab(piece, shift_y, 1)
                piece = take_slab(piece, shift_z, 2)
                cols_list.append(piece)
            rows_list.append(jnp.concatenate(cols_list, axis=2))
        planes.append(jnp.concatenate(rows_list, axis=1))
    padded_cube = jnp.concatenate(planes, axis=0)
    columns = []
    for shift_x in (-1, 0, 1):
        for shift_y in (-1, 0, 1):
            for shift_z in (-1, 0, 1):
                window = padded_cube[1 + shift_x:9 + shift_x, 1 + shift_y:9 + shift_y, 1 + shift_z:9 + shift_z]
                columns.append(window.reshape(512, channel_total))
    stack_cols = jnp.concatenate(columns, axis=1)
    return jnp.dot(stack_cols, conv_weight, preferred_element_type=jnp.float32)


def coarsen_blocks(fine_features, reduce_weight_matrix, channel_total):
    count = fine_features.shape[0]
    parts = fine_features.reshape(count, 4, 2, 4, 2, 4, 2, channel_total)
    parts = jnp.transpose(parts, (0, 1, 3, 5, 2, 4, 6, 7)).reshape(count, 64, 8 * channel_total)
    return jnp.einsum("bvc,co->bvo", parts.astype(jnp.float32), reduce_weight_matrix.astype(jnp.float32)).astype(jnp.bfloat16)


def reference(features, neighbour_table, send_lists, coarse_target, conv_weight, norm_gain, norm_shift, reduce_weight_matrix):
    channel_total = features.shape[2]
    nblocks = features.shape[0]
    empty_value = B_DEV + NOFF * HCAP
    device = (jnp.arange(nblocks, dtype=jnp.int32) // B_DEV)[:, None]
    entry = neighbour_table.astype(jnp.int32)
    local_id = device * B_DEV + entry
    halo_pos = jnp.clip(entry - B_DEV, 0, NOFF * HCAP - 1)
    offset_no = halo_pos // HCAP
    slot_no = halo_pos % HCAP
    distance = jnp.array(OFFSETS, dtype=jnp.int32)[offset_no]
    source = device - distance
    valid_src = (source >= 0) & (source < N_CELL)
    safe_src = jnp.clip(source, 0, N_CELL - 1)
    remote_id = safe_src * B_DEV + send_lists[safe_src, offset_no, slot_no].astype(jnp.int32)
    empty_id = jnp.full_like(entry, nblocks)
    global_id = jnp.where(entry < B_DEV, local_id, jnp.where((entry < empty_value) & valid_src, remote_id, empty_id))
    self_id = jnp.arange(nblocks, dtype=jnp.int32)[:, None]
    full_id = jnp.concatenate([global_id[:, :13], self_id, global_id[:, 13:]], axis=1)
    extended = jnp.concatenate([features, jnp.zeros((1, 512, channel_total), features.dtype)], axis=0)

    def one_block(ids):
        conv = conv_block(extended[ids], conv_weight, channel_total)
        return jnp.maximum(conv * norm_gain[None, :] + norm_shift[None, :], 0.0).astype(jnp.bfloat16)

    fine_output_features = lax.map(one_block, full_id)
    octant_list = coarsen_blocks(fine_output_features, reduce_weight_matrix, channel_total)
    target = coarse_target.astype(jnp.int32)
    block_dev = jnp.arange(nblocks, dtype=jnp.int32) // B_DEV
    owner = (block_dev // 2) * 2 + target // (8 * C_DEV)
    row = owner * (8 * C_DEV) + target % (8 * C_DEV)
    coarse_rows = jnp.zeros((N_CELL * C_DEV * 8, 64, channel_total), jnp.bfloat16).at[row].set(octant_list)
    coarse = coarse_rows.reshape(N_CELL * C_DEV, 2, 2, 2, 4, 4, 4, channel_total)
    coarse = jnp.transpose(coarse, (0, 1, 4, 2, 5, 3, 6, 7)).reshape(N_CELL * C_DEV, 512, channel_total)
    return fine_output_features, coarse
```

```python
import jax
import jax.numpy as jnp
import numpy as np
from jax import lax
from jax.experimental import pallas as pl
from jax.experimental.pallas import tpu as pltpu
from jax.sharding import PartitionSpec as P

OFFSETS = (1, -1, 2, -2)


def shifted(block, axis, distance):
    devices = range(lax.axis_size(axis))
    route = [(i - distance, i) for i in devices if i - distance in devices]
    return lax.ppermute(block, axis, route)


def swapped(block, axis):
    count = lax.axis_size(axis)
    return lax.ppermute(block, axis, [(i, i ^ 1) for i in range(count)])


def octant_order():
    order = np.zeros((128, 128), np.float32)
    for p in range(8):
        px, py, pz = p // 4, p // 2 % 2, p % 2
        for b in range(4):
            for c in range(4):
                order[p * 16 + b * 4 + c, px * 64 + (2 * b + py) * 8 + 2 * c + pz] = 1
    return jnp.asarray(order, jnp.bfloat16)


def coarse_order():
    order = np.zeros((64, 64), np.float32)
    for q in range(4):
        qy, qz = q // 2, q % 2
        for b in range(4):
            for c in range(4):
                order[(4 * qy + b) * 8 + 4 * qz + c, q * 16 + b * 4 + c] = 1
    return jnp.asarray(order, jnp.bfloat16)


def pick_kernel(lists, feats, out0, out1, out2, out3, sems):
    copies = []
    for i, out in enumerate((out0, out1, out2, out3)):
        for slot in range(out.shape[0]):
            copies.append(
                pltpu.make_async_copy(
                    feats.at[lists[i, slot]], out.at[slot], sems.at[i * out.shape[0] + slot]
                )
            )
    for copy in copies:
        copy.start()
    for copy in copies:
        copy.wait()


def fill_columns(g, ids, ext, cols):
    z = lax.broadcasted_iota(jnp.int32, (8, 8, 128), 1)

    def band(number, plane, oy):
        low, size = {-1: (48, 16), 0: (0, 64), 1: (0, 16)}[oy]
        rows = ext[ids[g, number], pl.ds(plane * 64 + low, size), :].astype(jnp.float32)
        rows = rows.reshape(size // 8, 8, 128)
        return {-1: rows[1:], 0: rows, 1: rows[:1]}[oy]

    def plane_of(place, ox, plane):
        bands = []
        for oy in (-1, 0, 1):
            first = 9 * (ox + 1) + 3 * (oy + 1)
            low, mid, high = (band(first + i, plane, oy) for i in range(3))
            mask = z[: mid.shape[0]]
            bands.append(
                (
                    pltpu.roll(jnp.where(mask == 7, low, mid), 1, 1),
                    mid,
                    pltpu.roll(jnp.where(mask == 0, high, mid), 7, 1),
                )
            )
        for kz in range(3):
            whole = jnp.concatenate([bands[0][kz], bands[1][kz], bands[2][kz]], axis=0)
            for ky in range(3):
                column = 3 * ky + kz
                cols[place, :, column * 128 : (column + 1) * 128] = (
                    whole[ky : ky + 8].reshape(64, 128).astype(jnp.bfloat16)
                )

    plane_of(0, -1, 7)
    for plane in range(8):
        plane_of(plane + 1, 0, plane)
    plane_of(9, 1, 0)


def conv_kernel(
    ids, feats, from0, from1, from2, from3, weight, gain, shift, reduce, order,
    fine, octant, ext, cols, grouped, sems,
):
    g = pl.program_id(0)
    blocks, slots = feats.shape[0], from0.shape[0]

    @pl.when(g == 0)
    def _():
        copies = [pltpu.make_async_copy(feats, ext.at[pl.ds(0, blocks)], sems.at[0])]
        for i, part in enumerate((from0, from1, from2, from3)):
            copies.append(
                pltpu.make_async_copy(
                    part, ext.at[pl.ds(blocks + i * slots, slots)], sems.at[i + 1]
                )
            )
        for copy in copies:
            copy.start()
        ext[blocks + 4 * slots] = jnp.zeros(ext.shape[1:], ext.dtype)
        for copy in copies:
            copy.wait()

    fill_columns(g, ids, ext, cols)
    total = None
    for kx in range(3):
        term = jnp.dot(
            cols[kx : kx + 8].reshape(512, 1152),
            weight[kx * 1152 : (kx + 1) * 1152],
            preferred_element_type=jnp.float32,
        )
        total = term if total is None else total + term
    out = jnp.maximum(total * gain[...] + shift[...], 0.0).astype(jnp.bfloat16)
    fine[0] = out
    for a in range(4):
        rows = jnp.dot(
            order[...], out[a * 128 : (a + 1) * 128], preferred_element_type=jnp.float32
        ).astype(jnp.bfloat16)
        for p in range(8):
            grouped[a * 16 : (a + 1) * 16, p * 128 : (p + 1) * 128] = rows[p * 16 : (p + 1) * 16]
    octant[0] = jnp.dot(
        grouped[...], reduce[...], preferred_element_type=jnp.float32
    ).astype(jnp.bfloat16)


def place_kernel(source, mine, other, order, coarse, rows, stack):
    count = mine.shape[0]
    rows[:count] = mine[...]
    rows[count : 2 * count] = other[...]
    rows[2 * count] = jnp.zeros(rows.shape[1:], rows.dtype)
    for slot in range(coarse.shape[0]):
        for qx in range(2):
            for a in range(4):
                for q in range(4):
                    stack[q * 16 : (q + 1) * 16] = rows[
                        source[slot * 8 + qx * 4 + q], a * 16 : (a + 1) * 16
                    ]
                start = (4 * qx + a) * 64
                coarse[slot, start : start + 64] = jnp.dot(
                    order[...], stack[...], preferred_element_type=jnp.float32
                ).astype(jnp.bfloat16)


def per_device(
    features,
    neighbour_table,
    send_lists,
    coarse_target,
    conv_weight,
    norm_gain,
    norm_shift,
    reduce_weight_matrix,
):
    blocks = features.shape[0]
    slots = send_lists.shape[2]
    channels = features.shape[2]
    myself = lax.axis_index("cell")
    vmem = pl.BlockSpec(memory_space=pltpu.VMEM)
    smem = pl.BlockSpec(memory_space=pltpu.SMEM)
    hbm = pl.BlockSpec(memory_space=pl.ANY)
    outgoing = pl.pallas_call(
        pick_kernel,
        in_specs=[smem, hbm],
        out_specs=[hbm] * 4,
        out_shape=[jax.ShapeDtypeStruct((slots, 512, channels), jnp.bfloat16)] * 4,
        scratch_shapes=[pltpu.SemaphoreType.DMA((4 * slots,))],
    )(send_lists[0], features)
    received = [shifted(part, "cell", d) for part, d in zip(outgoing, OFFSETS)]
    self_id = jnp.arange(blocks, dtype=jnp.int32)[:, None]
    ids = jnp.concatenate([neighbour_table[:, :13], self_id, neighbour_table[:, 13:]], axis=1)
    fine, octants = pl.pallas_call(
        conv_kernel,
        grid_spec=pltpu.PrefetchScalarGridSpec(
            num_scalar_prefetch=1,
            grid=(blocks,),
            in_specs=[hbm] * 5 + [vmem] * 5,
            out_specs=[
                pl.BlockSpec((1, 512, channels), lambda g, ids: (g, 0, 0)),
                pl.BlockSpec((1, 64, channels), lambda g, ids: (g, 0, 0)),
            ],
            scratch_shapes=[
                pltpu.VMEM((blocks + 4 * slots + 1, 512, channels), jnp.bfloat16),
                pltpu.VMEM((10, 64, 9 * channels), jnp.bfloat16),
                pltpu.VMEM((64, 8 * channels), jnp.bfloat16),
                pltpu.SemaphoreType.DMA((5,)),
            ],
        ),
        out_shape=[
            jax.ShapeDtypeStruct((blocks, 512, channels), jnp.bfloat16),
            jax.ShapeDtypeStruct((blocks, 64, channels), jnp.bfloat16),
        ],
        compiler_params=pltpu.CompilerParams(vmem_limit_bytes=40 * 1024 * 1024),
    )(
        ids, features, *received, conv_weight, norm_gain[None], norm_shift[None],
        reduce_weight_matrix, octant_order(),
    )
    partner_octants = swapped(octants, "cell")
    partner = jnp.bitwise_xor(myself, 1)
    targets = jnp.concatenate(
        [
            lax.dynamic_slice_in_dim(coarse_target, myself * blocks, blocks),
            lax.dynamic_slice_in_dim(coarse_target, partner * blocks, blocks),
        ]
    )
    coarse_slots = blocks // 4
    wanted = (myself % 2) * 8 * coarse_slots + jnp.arange(8 * coarse_slots, dtype=jnp.int32)
    hit = targets[None, :] == wanted[:, None]
    source = jnp.min(jnp.where(hit, jnp.arange(2 * blocks, dtype=jnp.int32), 2 * blocks), axis=1)
    coarse = pl.pallas_call(
        place_kernel,
        in_specs=[smem, vmem, vmem, vmem],
        out_specs=vmem,
        out_shape=jax.ShapeDtypeStruct((coarse_slots, 512, channels), jnp.bfloat16),
        scratch_shapes=[
            pltpu.VMEM((2 * blocks + 1, 64, channels), jnp.bfloat16),
            pltpu.VMEM((64, channels), jnp.bfloat16),
        ],
        compiler_params=pltpu.CompilerParams(vmem_limit_bytes=16 * 1024 * 1024),
    )(source.astype(jnp.int32), octants, partner_octants, coarse_order())
    return (fine, coarse)


def solution(mesh):
    return jax.shard_map(
        per_device,
        mesh=mesh,
        in_specs=(
            P(("groups", "cell"), None, None),
            P(("groups", "cell"), None),
            P(("groups", "cell"), None, None),
            P("groups"),
            P(),
            P(),
            P(),
            P(),
        ),
        out_specs=(P(("groups", "cell"), None, None), P(("groups", "cell"), None, None)),
        check_vma=False,
    )
```

```python
import jax
import jax.numpy as jnp
import numpy as np
from jax import lax
from jax.experimental import pallas as pl
from jax.experimental.pallas import tpu as pltpu
from jax.sharding import PartitionSpec as P

OFFSETS = (1, -1, 2, -2)


def shifted(block, axis, distance):
    devices = range(lax.axis_size(axis))
    route = [(i - distance, i) for i in devices if i - distance in devices]
    return lax.ppermute(block, axis, route)


def swapped(block, axis):
    count = lax.axis_size(axis)
    return lax.ppermute(block, axis, [(i, i ^ 1) for i in range(count)])


def octant_order():
    order = np.zeros((128, 128), np.float32)
    for p in range(8):
        px, py, pz = p // 4, p // 2 % 2, p % 2
        for b in range(4):
            for c in range(4):
                order[p * 16 + b * 4 + c, px * 64 + (2 * b + py) * 8 + 2 * c + pz] = 1
    return jnp.asarray(order, jnp.bfloat16)


def coarse_order():
    order = np.zeros((64, 64), np.float32)
    for q in range(4):
        qy, qz = q // 2, q % 2
        for b in range(4):
            for c in range(4):
                order[(4 * qy + b) * 8 + 4 * qz + c, q * 16 + b * 4 + c] = 1
    return jnp.asarray(order, jnp.bfloat16)


def pick_kernel(lists, feats, shell, out0, out1, out2, out3, wide):
    @pl.loop(0, feats.shape[0])
    def _(g):
        shell[g, :64] = feats[g, :64]
        shell[g, 64:128] = feats[g, 448:]
        wide[...] = feats[g].astype(jnp.float32)
        for a in range(1, 7):
            start = 128 + (a - 1) * 32
            lines = [
                wide[a * 64 : a * 64 + 8],
                wide[a * 64 + 56 : a * 64 + 64],
                wide[pl.ds(a * 64, 8, stride=8)],
                wide[pl.ds(a * 64 + 7, 8, stride=8)],
            ]
            shell[g, start : start + 32] = jnp.concatenate(lines).astype(jnp.bfloat16)

    for i, out in enumerate((out0, out1, out2, out3)):
        for slot in range(out.shape[0]):
            out[slot] = shell[lists[i, slot]]


def fill_columns(g, ids, own, ext, cols):
    z = lax.broadcasted_iota(jnp.int32, (8, 8, 128), 1)

    def rows_of(number, start, size):
        return ext[ids[g, number], start : start + size].astype(jnp.float32)

    def spread(line):
        return jnp.broadcast_to(line[:, None, :], (8, 8, 128))

    def shifts(low, mid, high):
        mask = z[: mid.shape[0]]
        return (
            pltpu.roll(jnp.where(mask == 7, low, mid), 1, 1),
            mid,
            pltpu.roll(jnp.where(mask == 0, high, mid), 7, 1),
        )

    def store(place, bands):
        for kz in range(3):
            whole = jnp.concatenate([bands[0][kz], bands[1][kz], bands[2][kz]], axis=0)
            for ky in range(3):
                column = 3 * ky + kz
                cols[place, :, column * 128 : (column + 1) * 128] = (
                    whole[ky : ky + 8].reshape(64, 128).astype(jnp.bfloat16)
                )

    def end_plane(place, ox, start):
        bands = []
        for oy in (-1, 0, 1):
            first = 9 * (ox + 1) + 3 * (oy + 1)
            low, size = {-1: (48, 16), 0: (0, 64), 1: (0, 16)}[oy]
            parts = []
            for i in range(3):
                part = rows_of(first + i, start + low, size).reshape(size // 8, 8, 128)
                parts.append({-1: part[1:], 0: part, 1: part[:1]}[oy])
            bands.append(shifts(*parts))
        store(place, bands)

    def inner_plane(a):
        def line(number, which):
            if a in (0, 7):
                start = 0 if a == 0 else 64
                if which < 2:
                    return rows_of(number, start + 48 * which, 16)[8 * which : 8 * which + 8]
                return rows_of(number, start, 64).reshape(8, 8, 128)
            rows = rows_of(number, 128 + (a - 1) * 32 + 16 * (which // 2), 16)
            return rows[8 * (which % 2) : 8 * (which % 2) + 8]

        mid = own[g, a * 64 : (a + 1) * 64].astype(jnp.float32).reshape(8, 8, 128)
        sides = [line(12, 3), line(14, 2)]
        if a not in (0, 7):
            sides = [spread(side) for side in sides]
        store(
            a + 1,
            [
                shifts(*(line(9 + i, 1)[None] for i in range(3))),
                shifts(sides[0], mid, sides[1]),
                shifts(*(line(15 + i, 0)[None] for i in range(3))),
            ],
        )

    end_plane(0, -1, 64)
    for a in range(8):
        inner_plane(a)
    end_plane(9, 1, 0)


def conv_kernel(
    ids, own, feats, from0, from1, from2, from3, weight, gain, shift, reduce, order,
    fine, octant, ext, cols, grouped, sems,
):
    g = pl.program_id(0)
    blocks, slots = feats.shape[0], from0.shape[0]

    @pl.when(g == 0)
    def _():
        copies = [pltpu.make_async_copy(feats, ext.at[pl.ds(0, blocks)], sems.at[0])]
        for i, part in enumerate((from0, from1, from2, from3)):
            copies.append(
                pltpu.make_async_copy(
                    part, ext.at[pl.ds(blocks + i * slots, slots)], sems.at[i + 1]
                )
            )
        for copy in copies:
            copy.start()
        ext[blocks + 4 * slots] = jnp.zeros(ext.shape[1:], ext.dtype)
        for copy in copies:
            copy.wait()

    fill_columns(g, ids, own, ext, cols)
    total = None
    for kx in range(3):
        term = jnp.dot(
            cols[kx : kx + 8].reshape(512, 1152),
            weight[kx * 1152 : (kx + 1) * 1152],
            preferred_element_type=jnp.float32,
        )
        total = term if total is None else total + term
    out = jnp.maximum(total * gain[...] + shift[...], 0.0).astype(jnp.bfloat16)
    fine[0] = out
    for a in range(4):
        rows = jnp.dot(
            order[...], out[a * 128 : (a + 1) * 128], preferred_element_type=jnp.float32
        ).astype(jnp.bfloat16)
        for p in range(8):
            grouped[a * 16 : (a + 1) * 16, p * 128 : (p + 1) * 128] = rows[p * 16 : (p + 1) * 16]
    octant[0] = jnp.dot(
        grouped[...], reduce[...], preferred_element_type=jnp.float32
    ).astype(jnp.bfloat16)


def place_kernel(source, mine, other, order, coarse, rows, stack):
    count = mine.shape[0]
    rows[:count] = mine[...]
    rows[count : 2 * count] = other[...]
    rows[2 * count] = jnp.zeros(rows.shape[1:], rows.dtype)
    for slot in range(coarse.shape[0]):
        for qx in range(2):
            for a in range(4):
                for q in range(4):
                    stack[q * 16 : (q + 1) * 16] = rows[
                        source[slot * 8 + qx * 4 + q], a * 16 : (a + 1) * 16
                    ]
                start = (4 * qx + a) * 64
                coarse[slot, start : start + 64] = jnp.dot(
                    order[...], stack[...], preferred_element_type=jnp.float32
                ).astype(jnp.bfloat16)


def per_device(
    features,
    neighbour_table,
    send_lists,
    coarse_target,
    conv_weight,
    norm_gain,
    norm_shift,
    reduce_weight_matrix,
):
    blocks = features.shape[0]
    slots = send_lists.shape[2]
    channels = features.shape[2]
    myself = lax.axis_index("cell")
    vmem = pl.BlockSpec(memory_space=pltpu.VMEM)
    smem = pl.BlockSpec(memory_space=pltpu.SMEM)
    hbm = pl.BlockSpec(memory_space=pl.ANY)
    rows = 320
    shell, *outgoing = pl.pallas_call(
        pick_kernel,
        in_specs=[smem, vmem],
        out_specs=[vmem] * 5,
        out_shape=[jax.ShapeDtypeStruct((blocks, rows, channels), jnp.bfloat16)]
        + [jax.ShapeDtypeStruct((slots, rows, channels), jnp.bfloat16)] * 4,
        scratch_shapes=[pltpu.VMEM((512, channels), jnp.float32)],
        compiler_params=pltpu.CompilerParams(vmem_limit_bytes=16 * 1024 * 1024),
    )(send_lists[0], features)
    received = [shifted(part, "cell", d) for part, d in zip(outgoing, OFFSETS)]
    self_id = jnp.arange(blocks, dtype=jnp.int32)[:, None]
    ids = jnp.concatenate([neighbour_table[:, :13], self_id, neighbour_table[:, 13:]], axis=1)
    fine, octants = pl.pallas_call(
        conv_kernel,
        grid_spec=pltpu.PrefetchScalarGridSpec(
            num_scalar_prefetch=1,
            grid=(blocks,),
            in_specs=[vmem] + [hbm] * 5 + [vmem] * 5,
            out_specs=[
                pl.BlockSpec((1, 512, channels), lambda g, ids: (g, 0, 0)),
                pl.BlockSpec((1, 64, channels), lambda g, ids: (g, 0, 0)),
            ],
            scratch_shapes=[
                pltpu.VMEM((blocks + 4 * slots + 1, rows, channels), jnp.bfloat16),
                pltpu.VMEM((10, 64, 9 * channels), jnp.bfloat16),
                pltpu.VMEM((64, 8 * channels), jnp.bfloat16),
                pltpu.SemaphoreType.DMA((5,)),
            ],
        ),
        out_shape=[
            jax.ShapeDtypeStruct((blocks, 512, channels), jnp.bfloat16),
            jax.ShapeDtypeStruct((blocks, 64, channels), jnp.bfloat16),
        ],
        compiler_params=pltpu.CompilerParams(vmem_limit_bytes=40 * 1024 * 1024),
    )(
        ids, features, shell, *received, conv_weight, norm_gain[None], norm_shift[None],
        reduce_weight_matrix, octant_order(),
    )
    partner_octants = swapped(octants, "cell")
    partner = jnp.bitwise_xor(myself, 1)
    targets = jnp.concatenate(
        [
            lax.dynamic_slice_in_dim(coarse_target, myself * blocks, blocks),
            lax.dynamic_slice_in_dim(coarse_target, partner * blocks, blocks),
        ]
    )
    coarse_slots = blocks // 4
    wanted = (myself % 2) * 8 * coarse_slots + jnp.arange(8 * coarse_slots, dtype=jnp.int32)
    hit = targets[None, :] == wanted[:, None]
    source = jnp.min(jnp.where(hit, jnp.arange(2 * blocks, dtype=jnp.int32), 2 * blocks), axis=1)
    coarse = pl.pallas_call(
        place_kernel,
        in_specs=[smem, vmem, vmem, vmem],
        out_specs=vmem,
        out_shape=jax.ShapeDtypeStruct((coarse_slots, 512, channels), jnp.bfloat16),
        scratch_shapes=[
            pltpu.VMEM((2 * blocks + 1, 64, channels), jnp.bfloat16),
            pltpu.VMEM((64, channels), jnp.bfloat16),
        ],
        compiler_params=pltpu.CompilerParams(vmem_limit_bytes=16 * 1024 * 1024),
    )(source.astype(jnp.int32), octants, partner_octants, coarse_order())
    return (fine, coarse)


def solution(mesh):
    return jax.shard_map(
        per_device,
        mesh=mesh,
        in_specs=(
            P(("groups", "cell"), None, None),
            P(("groups", "cell"), None),
            P(("groups", "cell"), None, None),
            P("groups"),
            P(),
            P(),
            P(),
            P(),
        ),
        out_specs=(P(("groups", "cell"), None, None), P(("groups", "cell"), None, None)),
        check_vma=False,
    )
```

```python
import jax
import jax.numpy as jnp
import numpy as np
from jax import lax
from jax.experimental import pallas as pl
from jax.experimental.pallas import tpu as pltpu
from jax.sharding import PartitionSpec as P

OFFSETS = (1, -1, 2, -2)


def swapped(block, axis):
    count = lax.axis_size(axis)
    return lax.ppermute(block, axis, [(i, i ^ 1) for i in range(count)])


def octant_order():
    order = np.zeros((128, 128), np.float32)
    for p in range(8):
        px, py, pz = p // 4, p // 2 % 2, p % 2
        for b in range(4):
            for c in range(4):
                order[p * 16 + b * 4 + c, px * 64 + (2 * b + py) * 8 + 2 * c + pz] = 1
    return jnp.asarray(order, jnp.bfloat16)


def coarse_order():
    order = np.zeros((64, 64), np.float32)
    for q in range(4):
        qy, qz = q // 2, q % 2
        for b in range(4):
            for c in range(4):
                order[(4 * qy + b) * 8 + 4 * qz + c, q * 16 + b * 4 + c] = 1
    return jnp.asarray(order, jnp.bfloat16)


def exchange_kernel(
    lists, feats, shell, in0, in1, in2, in3, wide, out0, out1, out2, out3, sent, landed
):
    me, count = lax.axis_index("cell"), lax.axis_size("cell")
    barrier = pltpu.get_barrier_semaphore()

    def there(device):
        return (device >= 0) & (device < count)

    for d in OFFSETS:

        @pl.when(there(me + d))
        def _(d=d):
            pl.semaphore_signal(
                barrier, inc=1, device_id={"cell": me + d}, device_id_type=pl.DeviceIdType.MESH
            )

    @pl.loop(0, feats.shape[0])
    def _(g):
        shell[g, :64] = feats[g, :64]
        shell[g, 64:128] = feats[g, 448:]
        wide[...] = feats[g].astype(jnp.float32)
        for a in range(1, 7):
            start = 128 + (a - 1) * 32
            lines = [
                wide[a * 64 : a * 64 + 8],
                wide[a * 64 + 56 : a * 64 + 64],
                wide[pl.ds(a * 64, 8, stride=8)],
                wide[pl.ds(a * 64 + 7, 8, stride=8)],
            ]
            shell[g, start : start + 32] = jnp.concatenate(lines).astype(jnp.bfloat16)

    for i, out in enumerate((out0, out1, out2, out3)):
        for slot in range(out.shape[0]):
            out[slot] = shell[lists[i, slot]]

    pl.semaphore_wait(barrier, sum(there(me + d).astype(jnp.int32) for d in OFFSETS))

    copies = []
    for i, (d, out, into) in enumerate(
        zip(OFFSETS, (out0, out1, out2, out3), (in0, in1, in2, in3))
    ):
        copy = pltpu.make_async_remote_copy(
            src_ref=out,
            dst_ref=into,
            send_sem=sent.at[i],
            recv_sem=landed.at[i],
            device_id={"cell": me + d},
            device_id_type=pl.DeviceIdType.MESH,
        )
        copies.append(copy)
        pl.when(there(me + d))(copy.start)
    for d, into, copy in zip(OFFSETS, (in0, in1, in2, in3), copies):

        @pl.when(there(me - d))
        def _(copy=copy):
            copy.wait_recv()

        @pl.when(jnp.logical_not(there(me - d)))
        def _(into=into):
            into[...] = jnp.zeros_like(into)

        @pl.when(there(me + d))
        def _(copy=copy):
            copy.wait_send()


def fill_columns(g, ids, own, ext, cols):
    z = lax.broadcasted_iota(jnp.int32, (8, 8, 128), 1)

    def rows_of(number, start, size):
        return ext[ids[g, number], start : start + size].astype(jnp.float32)

    def spread(line):
        return jnp.broadcast_to(line[:, None, :], (8, 8, 128))

    def shifts(low, mid, high):
        mask = z[: mid.shape[0]]
        return (
            pltpu.roll(jnp.where(mask == 7, low, mid), 1, 1),
            mid,
            pltpu.roll(jnp.where(mask == 0, high, mid), 7, 1),
        )

    def store(place, bands):
        for kz in range(3):
            whole = jnp.concatenate([bands[0][kz], bands[1][kz], bands[2][kz]], axis=0)
            for ky in range(3):
                column = 3 * ky + kz
                cols[place, :, column * 128 : (column + 1) * 128] = (
                    whole[ky : ky + 8].reshape(64, 128).astype(jnp.bfloat16)
                )

    def end_plane(place, ox, start):
        bands = []
        for oy in (-1, 0, 1):
            first = 9 * (ox + 1) + 3 * (oy + 1)
            low, size = {-1: (48, 16), 0: (0, 64), 1: (0, 16)}[oy]
            parts = []
            for i in range(3):
                part = rows_of(first + i, start + low, size).reshape(size // 8, 8, 128)
                parts.append({-1: part[1:], 0: part, 1: part[:1]}[oy])
            bands.append(shifts(*parts))
        store(place, bands)

    def inner_plane(a):
        def line(number, which):
            if a in (0, 7):
                start = 0 if a == 0 else 64
                if which < 2:
                    return rows_of(number, start + 48 * which, 16)[8 * which : 8 * which + 8]
                return rows_of(number, start, 64).reshape(8, 8, 128)
            rows = rows_of(number, 128 + (a - 1) * 32 + 16 * (which // 2), 16)
            return rows[8 * (which % 2) : 8 * (which % 2) + 8]

        mid = own[g, a * 64 : (a + 1) * 64].astype(jnp.float32).reshape(8, 8, 128)
        sides = [line(12, 3), line(14, 2)]
        if a not in (0, 7):
            sides = [spread(side) for side in sides]
        store(
            a + 1,
            [
                shifts(*(line(9 + i, 1)[None] for i in range(3))),
                shifts(sides[0], mid, sides[1]),
                shifts(*(line(15 + i, 0)[None] for i in range(3))),
            ],
        )

    end_plane(0, -1, 64)
    for a in range(8):
        inner_plane(a)
    end_plane(9, 1, 0)


def conv_kernel(
    ids, own, feats, from0, from1, from2, from3, weight, gain, shift, reduce, order,
    fine, octant, ext, cols, grouped, sems,
):
    g = pl.program_id(0)
    blocks, slots = feats.shape[0], from0.shape[0]

    @pl.when(g == 0)
    def _():
        copies = [pltpu.make_async_copy(feats, ext.at[pl.ds(0, blocks)], sems.at[0])]
        for i, part in enumerate((from0, from1, from2, from3)):
            copies.append(
                pltpu.make_async_copy(
                    part, ext.at[pl.ds(blocks + i * slots, slots)], sems.at[i + 1]
                )
            )
        for copy in copies:
            copy.start()
        ext[blocks + 4 * slots] = jnp.zeros(ext.shape[1:], ext.dtype)
        for copy in copies:
            copy.wait()

    fill_columns(g, ids, own, ext, cols)
    total = None
    for kx in range(3):
        term = jnp.dot(
            cols[kx : kx + 8].reshape(512, 1152),
            weight[kx * 1152 : (kx + 1) * 1152],
            preferred_element_type=jnp.float32,
        )
        total = term if total is None else total + term
    out = jnp.maximum(total * gain[...] + shift[...], 0.0).astype(jnp.bfloat16)
    fine[0] = out
    for a in range(4):
        rows = jnp.dot(
            order[...], out[a * 128 : (a + 1) * 128], preferred_element_type=jnp.float32
        ).astype(jnp.bfloat16)
        for p in range(8):
            grouped[a * 16 : (a + 1) * 16, p * 128 : (p + 1) * 128] = rows[p * 16 : (p + 1) * 16]
    octant[0] = jnp.dot(
        grouped[...], reduce[...], preferred_element_type=jnp.float32
    ).astype(jnp.bfloat16)


def place_kernel(source, mine, other, order, coarse, rows, stack):
    count = mine.shape[0]
    rows[:count] = mine[...]
    rows[count : 2 * count] = other[...]
    rows[2 * count] = jnp.zeros(rows.shape[1:], rows.dtype)
    for slot in range(coarse.shape[0]):
        for qx in range(2):
            for a in range(4):
                for q in range(4):
                    stack[q * 16 : (q + 1) * 16] = rows[
                        source[slot * 8 + qx * 4 + q], a * 16 : (a + 1) * 16
                    ]
                start = (4 * qx + a) * 64
                coarse[slot, start : start + 64] = jnp.dot(
                    order[...], stack[...], preferred_element_type=jnp.float32
                ).astype(jnp.bfloat16)


def per_device(
    features,
    neighbour_table,
    send_lists,
    coarse_target,
    conv_weight,
    norm_gain,
    norm_shift,
    reduce_weight_matrix,
):
    blocks = features.shape[0]
    slots = send_lists.shape[2]
    channels = features.shape[2]
    myself = lax.axis_index("cell")
    vmem = pl.BlockSpec(memory_space=pltpu.VMEM)
    smem = pl.BlockSpec(memory_space=pltpu.SMEM)
    hbm = pl.BlockSpec(memory_space=pl.ANY)
    rows = 320
    shell, *received = pl.pallas_call(
        exchange_kernel,
        in_specs=[smem, vmem],
        out_specs=[vmem] * 5,
        out_shape=[jax.ShapeDtypeStruct((blocks, rows, channels), jnp.bfloat16)]
        + [jax.ShapeDtypeStruct((slots, rows, channels), jnp.bfloat16)] * 4,
        scratch_shapes=[pltpu.VMEM((512, channels), jnp.float32)]
        + [pltpu.VMEM((slots, rows, channels), jnp.bfloat16)] * 4
        + [pltpu.SemaphoreType.DMA((4,)), pltpu.SemaphoreType.DMA((4,))],
        compiler_params=pltpu.CompilerParams(
            vmem_limit_bytes=24 * 1024 * 1024, collective_id=0, has_side_effects=True
        ),
    )(send_lists[0], features)
    self_id = jnp.arange(blocks, dtype=jnp.int32)[:, None]
    ids = jnp.concatenate([neighbour_table[:, :13], self_id, neighbour_table[:, 13:]], axis=1)
    fine, octants = pl.pallas_call(
        conv_kernel,
        grid_spec=pltpu.PrefetchScalarGridSpec(
            num_scalar_prefetch=1,
            grid=(blocks,),
            in_specs=[vmem] + [hbm] * 5 + [vmem] * 5,
            out_specs=[
                pl.BlockSpec((1, 512, channels), lambda g, ids: (g, 0, 0)),
                pl.BlockSpec((1, 64, channels), lambda g, ids: (g, 0, 0)),
            ],
            scratch_shapes=[
                pltpu.VMEM((blocks + 4 * slots + 1, rows, channels), jnp.bfloat16),
                pltpu.VMEM((10, 64, 9 * channels), jnp.bfloat16),
                pltpu.VMEM((64, 8 * channels), jnp.bfloat16),
                pltpu.SemaphoreType.DMA((5,)),
            ],
        ),
        out_shape=[
            jax.ShapeDtypeStruct((blocks, 512, channels), jnp.bfloat16),
            jax.ShapeDtypeStruct((blocks, 64, channels), jnp.bfloat16),
        ],
        compiler_params=pltpu.CompilerParams(vmem_limit_bytes=40 * 1024 * 1024),
    )(
        ids, features, shell, *received, conv_weight, norm_gain[None], norm_shift[None],
        reduce_weight_matrix, octant_order(),
    )
    partner_octants = swapped(octants, "cell")
    partner = jnp.bitwise_xor(myself, 1)
    targets = jnp.concatenate(
        [
            lax.dynamic_slice_in_dim(coarse_target, myself * blocks, blocks),
            lax.dynamic_slice_in_dim(coarse_target, partner * blocks, blocks),
        ]
    )
    coarse_slots = blocks // 4
    wanted = (myself % 2) * 8 * coarse_slots + jnp.arange(8 * coarse_slots, dtype=jnp.int32)
    hit = targets[None, :] == wanted[:, None]
    source = jnp.min(jnp.where(hit, jnp.arange(2 * blocks, dtype=jnp.int32), 2 * blocks), axis=1)
    coarse = pl.pallas_call(
        place_kernel,
        in_specs=[smem, vmem, vmem, vmem],
        out_specs=vmem,
        out_shape=jax.ShapeDtypeStruct((coarse_slots, 512, channels), jnp.bfloat16),
        scratch_shapes=[
            pltpu.VMEM((2 * blocks + 1, 64, channels), jnp.bfloat16),
            pltpu.VMEM((64, channels), jnp.bfloat16),
        ],
        compiler_params=pltpu.CompilerParams(vmem_limit_bytes=16 * 1024 * 1024),
    )(source.astype(jnp.int32), octants, partner_octants, coarse_order())
    return (fine, coarse)


def solution(mesh):
    return jax.shard_map(
        per_device,
        mesh=mesh,
        in_specs=(
            P(("groups", "cell"), None, None),
            P(("groups", "cell"), None),
            P(("groups", "cell"), None, None),
            P("groups"),
            P(),
            P(),
            P(),
            P(),
        ),
        out_specs=(P(("groups", "cell"), None, None), P(("groups", "cell"), None, None)),
        check_vma=False,
    )
```

```python
import jax
import jax.numpy as jnp
import numpy as np
from jax import lax
from jax.experimental import pallas as pl
from jax.experimental.pallas import tpu as pltpu
from jax.sharding import PartitionSpec as P

OFFSETS = (1, -1, 2, -2)


def swapped(block, axis):
    count = lax.axis_size(axis)
    return lax.ppermute(block, axis, [(i, i ^ 1) for i in range(count)])


def octant_order():
    order = np.zeros((128, 128), np.float32)
    for p in range(8):
        px, py, pz = p // 4, p // 2 % 2, p % 2
        for b in range(4):
            for c in range(4):
                order[p * 16 + b * 4 + c, px * 64 + (2 * b + py) * 8 + 2 * c + pz] = 1
    return jnp.asarray(order, jnp.bfloat16)


def coarse_order():
    order = np.zeros((64, 64), np.float32)
    for q in range(4):
        qy, qz = q // 2, q % 2
        for b in range(4):
            for c in range(4):
                order[(4 * qy + b) * 8 + 4 * qz + c, q * 16 + b * 4 + c] = 1
    return jnp.asarray(order, jnp.bfloat16)


def exchange_kernel(
    lists, feats, shell, in0, in1, in2, in3, wide, out0, out1, out2, out3, sent, landed
):
    me, count = lax.axis_index("cell"), lax.axis_size("cell")
    barrier = pltpu.get_barrier_semaphore()

    def there(device):
        return (device >= 0) & (device < count)

    for d in OFFSETS:

        @pl.when(there(me + d))
        def _(d=d):
            pl.semaphore_signal(
                barrier, inc=1, device_id={"cell": me + d}, device_id_type=pl.DeviceIdType.MESH
            )

    @pl.loop(0, feats.shape[0])
    def _(g):
        shell[g, :64] = feats[g, :64]
        shell[g, 64:128] = feats[g, 448:]
        wide[...] = feats[g].astype(jnp.float32)
        for a in range(1, 7):
            start = 128 + (a - 1) * 32
            lines = [
                wide[a * 64 : a * 64 + 8],
                wide[a * 64 + 56 : a * 64 + 64],
                wide[pl.ds(a * 64, 8, stride=8)],
                wide[pl.ds(a * 64 + 7, 8, stride=8)],
            ]
            shell[g, start : start + 32] = jnp.concatenate(lines).astype(jnp.bfloat16)

    for i, out in enumerate((out0, out1, out2, out3)):
        for slot in range(out.shape[0]):
            out[slot] = shell[lists[i, slot]]

    pl.semaphore_wait(barrier, sum(there(me + d).astype(jnp.int32) for d in OFFSETS))

    copies = []
    for i, (d, out, into) in enumerate(
        zip(OFFSETS, (out0, out1, out2, out3), (in0, in1, in2, in3))
    ):
        copy = pltpu.make_async_remote_copy(
            src_ref=out,
            dst_ref=into,
            send_sem=sent.at[i],
            recv_sem=landed.at[i],
            device_id={"cell": me + d},
            device_id_type=pl.DeviceIdType.MESH,
        )
        copies.append(copy)
        pl.when(there(me + d))(copy.start)
    for d, into, copy in zip(OFFSETS, (in0, in1, in2, in3), copies):

        @pl.when(there(me - d))
        def _(copy=copy):
            copy.wait_recv()

        @pl.when(jnp.logical_not(there(me - d)))
        def _(into=into):
            into[...] = jnp.zeros_like(into)

        @pl.when(there(me + d))
        def _(copy=copy):
            copy.wait_send()


def fill_columns(g, ids, own, ext, cols):
    z = lax.broadcasted_iota(jnp.int32, (8, 8, 128), 1)

    def rows_of(number, start, size):
        return ext[ids[g, number - (number > 13)], start : start + size].astype(jnp.float32)

    def spread(line):
        return jnp.broadcast_to(line[:, None, :], (8, 8, 128))

    def shifts(low, mid, high):
        mask = z[: mid.shape[0]]
        return (
            pltpu.roll(jnp.where(mask == 7, low, mid), 1, 1),
            mid,
            pltpu.roll(jnp.where(mask == 0, high, mid), 7, 1),
        )

    def store(place, bands):
        for kz in range(3):
            whole = jnp.concatenate([bands[0][kz], bands[1][kz], bands[2][kz]], axis=0)
            for ky in range(3):
                column = 3 * ky + kz
                cols[place, :, column * 128 : (column + 1) * 128] = (
                    whole[ky : ky + 8].reshape(64, 128).astype(jnp.bfloat16)
                )

    def end_plane(place, ox, start):
        bands = []
        for oy in (-1, 0, 1):
            first = 9 * (ox + 1) + 3 * (oy + 1)
            low, size = {-1: (48, 16), 0: (0, 64), 1: (0, 16)}[oy]
            parts = []
            for i in range(3):
                part = rows_of(first + i, start + low, size).reshape(size // 8, 8, 128)
                parts.append({-1: part[1:], 0: part, 1: part[:1]}[oy])
            bands.append(shifts(*parts))
        store(place, bands)

    def inner_plane(a):
        def line(number, which):
            if a in (0, 7):
                start = 0 if a == 0 else 64
                if which < 2:
                    return rows_of(number, start + 48 * which, 16)[8 * which : 8 * which + 8]
                return rows_of(number, start, 64).reshape(8, 8, 128)
            rows = rows_of(number, 128 + (a - 1) * 32 + 16 * (which // 2), 16)
            return rows[8 * (which % 2) : 8 * (which % 2) + 8]

        mid = own[g, a * 64 : (a + 1) * 64].astype(jnp.float32).reshape(8, 8, 128)
        sides = [line(12, 3), line(14, 2)]
        if a not in (0, 7):
            sides = [spread(side) for side in sides]
        store(
            a + 1,
            [
                shifts(*(line(9 + i, 1)[None] for i in range(3))),
                shifts(sides[0], mid, sides[1]),
                shifts(*(line(15 + i, 0)[None] for i in range(3))),
            ],
        )

    end_plane(0, -1, 64)
    for a in range(8):
        inner_plane(a)
    end_plane(9, 1, 0)


def conv_kernel(
    ids, own, feats, from0, from1, from2, from3, weight, gain, shift, reduce, order,
    fine, octant, ext, even, odd, grouped, sems,
):
    g = pl.program_id(0)
    blocks, slots = feats.shape[0], from0.shape[0]

    @pl.when(g == 0)
    def _():
        copies = [pltpu.make_async_copy(feats, ext.at[pl.ds(0, blocks)], sems.at[0])]
        for i, part in enumerate((from0, from1, from2, from3)):
            copies.append(
                pltpu.make_async_copy(
                    part, ext.at[pl.ds(blocks + i * slots, slots)], sems.at[i + 1]
                )
            )
        for copy in copies:
            copy.start()
        ext[blocks + 4 * slots] = jnp.zeros(ext.shape[1:], ext.dtype)
        for copy in copies:
            copy.wait()

    def finish(slot, cols):
        total = None
        for kx in range(3):
            term = jnp.dot(
                cols[kx : kx + 8].reshape(512, 1152),
                weight[kx * 1152 : (kx + 1) * 1152],
                preferred_element_type=jnp.float32,
            )
            total = term if total is None else total + term
        out = jnp.maximum(total * gain[...] + shift[...], 0.0).astype(jnp.bfloat16)
        fine[slot] = out
        for a in range(4):
            rows = jnp.dot(
                order[...], out[a * 128 : (a + 1) * 128], preferred_element_type=jnp.float32
            ).astype(jnp.bfloat16)
            for p in range(8):
                grouped[slot, a * 16 : (a + 1) * 16, p * 128 : (p + 1) * 128] = rows[
                    p * 16 : (p + 1) * 16
                ]
        octant[slot] = jnp.dot(
            grouped[slot], reduce[...], preferred_element_type=jnp.float32
        ).astype(jnp.bfloat16)

    pl.when(g == 0)(lambda: fill_columns(0, ids, own, ext, even))
    fill_columns(2 * g + 1, ids, own, ext, odd)
    finish(0, even)
    fill_columns(jnp.minimum(2 * g + 2, blocks - 2), ids, own, ext, even)
    finish(1, odd)


def place_kernel(source, mine, other, order, coarse, rows, stack):
    count = mine.shape[0]
    rows[:count] = mine[...]
    rows[count : 2 * count] = other[...]
    rows[2 * count] = jnp.zeros(rows.shape[1:], rows.dtype)
    for slot in range(coarse.shape[0]):
        for qx in range(2):
            for a in range(4):
                for q in range(4):
                    stack[q * 16 : (q + 1) * 16] = rows[
                        source[slot * 8 + qx * 4 + q], a * 16 : (a + 1) * 16
                    ]
                start = (4 * qx + a) * 64
                coarse[slot, start : start + 64] = jnp.dot(
                    order[...], stack[...], preferred_element_type=jnp.float32
                ).astype(jnp.bfloat16)


def per_device(
    features,
    neighbour_table,
    send_lists,
    coarse_target,
    conv_weight,
    norm_gain,
    norm_shift,
    reduce_weight_matrix,
):
    blocks = features.shape[0]
    slots = send_lists.shape[2]
    channels = features.shape[2]
    myself = lax.axis_index("cell")
    vmem = pl.BlockSpec(memory_space=pltpu.VMEM)
    smem = pl.BlockSpec(memory_space=pltpu.SMEM)
    hbm = pl.BlockSpec(memory_space=pl.ANY)
    rows = 320
    shell, *received = pl.pallas_call(
        exchange_kernel,
        in_specs=[smem, vmem],
        out_specs=[vmem] * 5,
        out_shape=[jax.ShapeDtypeStruct((blocks, rows, channels), jnp.bfloat16)]
        + [jax.ShapeDtypeStruct((slots, rows, channels), jnp.bfloat16)] * 4,
        scratch_shapes=[pltpu.VMEM((512, channels), jnp.float32)]
        + [pltpu.VMEM((slots, rows, channels), jnp.bfloat16)] * 4
        + [pltpu.SemaphoreType.DMA((4,)), pltpu.SemaphoreType.DMA((4,))],
        cost_estimate=pl.CostEstimate(flops=0, bytes_accessed=60_000_000, transcendentals=0),
        compiler_params=pltpu.CompilerParams(
            vmem_limit_bytes=24 * 1024 * 1024, collective_id=0, has_side_effects=True
        ),
    )(send_lists[0], features)
    fine, octants = pl.pallas_call(
        conv_kernel,
        grid_spec=pltpu.PrefetchScalarGridSpec(
            num_scalar_prefetch=1,
            grid=(blocks // 2,),
            in_specs=[vmem] + [hbm] * 5 + [vmem] * 5,
            out_specs=[
                pl.BlockSpec((2, 512, channels), lambda g, ids: (g, 0, 0)),
                pl.BlockSpec((2, 64, channels), lambda g, ids: (g, 0, 0)),
            ],
            scratch_shapes=[
                pltpu.VMEM((blocks + 4 * slots + 1, rows, channels), jnp.bfloat16),
                pltpu.VMEM((10, 64, 9 * channels), jnp.bfloat16),
                pltpu.VMEM((10, 64, 9 * channels), jnp.bfloat16),
                pltpu.VMEM((2, 64, 8 * channels), jnp.bfloat16),
                pltpu.SemaphoreType.DMA((5,)),
            ],
        ),
        out_shape=[
            jax.ShapeDtypeStruct((blocks, 512, channels), jnp.bfloat16),
            jax.ShapeDtypeStruct((blocks, 64, channels), jnp.bfloat16),
        ],
        cost_estimate=pl.CostEstimate(
            flops=2 * blocks * 512 * conv_weight.shape[0] * channels,
            bytes_accessed=30_000_000,
            transcendentals=0,
        ),
        compiler_params=pltpu.CompilerParams(vmem_limit_bytes=40 * 1024 * 1024),
    )(
        neighbour_table, features, shell, *received, conv_weight, norm_gain[None], norm_shift[None],
        reduce_weight_matrix, octant_order(),
    )
    partner_octants = swapped(octants, "cell")
    partner = jnp.bitwise_xor(myself, 1)
    targets = jnp.concatenate(
        [
            lax.dynamic_slice_in_dim(coarse_target, myself * blocks, blocks),
            lax.dynamic_slice_in_dim(coarse_target, partner * blocks, blocks),
        ]
    )
    coarse_slots = blocks // 4
    wanted = (myself % 2) * 8 * coarse_slots + jnp.arange(8 * coarse_slots, dtype=jnp.int32)
    hit = targets[None, :] == wanted[:, None]
    source = jnp.min(jnp.where(hit, jnp.arange(2 * blocks, dtype=jnp.int32), 2 * blocks), axis=1)
    coarse = pl.pallas_call(
        place_kernel,
        in_specs=[smem, vmem, vmem, vmem],
        out_specs=vmem,
        out_shape=jax.ShapeDtypeStruct((coarse_slots, 512, channels), jnp.bfloat16),
        scratch_shapes=[
            pltpu.VMEM((2 * blocks + 1, 64, channels), jnp.bfloat16),
            pltpu.VMEM((64, channels), jnp.bfloat16),
        ],
        compiler_params=pltpu.CompilerParams(vmem_limit_bytes=16 * 1024 * 1024),
    )(source.astype(jnp.int32), octants, partner_octants, coarse_order())
    return (fine, coarse)


def solution(mesh):
    return jax.shard_map(
        per_device,
        mesh=mesh,
        in_specs=(
            P(("groups", "cell"), None, None),
            P(("groups", "cell"), None),
            P(("groups", "cell"), None, None),
            P("groups"),
            P(),
            P(),
            P(),
            P(),
        ),
        out_specs=(P(("groups", "cell"), None, None), P(("groups", "cell"), None, None)),
        check_vma=False,
    )
```

```python
import jax
import jax.numpy as jnp
import numpy as np
from jax import lax
from jax.experimental import pallas as pl
from jax.experimental.pallas import tpu as pltpu
from jax.sharding import PartitionSpec as P

OFFSETS = (1, -1, 2, -2)


def swapped(block, axis):
    count = lax.axis_size(axis)
    return lax.ppermute(block, axis, [(i, i ^ 1) for i in range(count)])


def octant_order():
    order = np.zeros((128, 128), np.float32)
    for p in range(8):
        px, py, pz = p // 4, p // 2 % 2, p % 2
        for b in range(4):
            for c in range(4):
                order[p * 16 + b * 4 + c, px * 64 + (2 * b + py) * 8 + 2 * c + pz] = 1
    return jnp.asarray(order, jnp.bfloat16)


def coarse_order():
    order = np.zeros((64, 64), np.float32)
    for q in range(4):
        qy, qz = q // 2, q % 2
        for b in range(4):
            for c in range(4):
                order[(4 * qy + b) * 8 + 4 * qz + c, q * 16 + b * 4 + c] = 1
    return jnp.asarray(order, jnp.bfloat16)


def exchange_kernel(
    lists, feats, shell, in0, in1, in2, in3, wide, out0, out1, out2, out3, sent, landed
):
    me, count = lax.axis_index("cell"), lax.axis_size("cell")
    barrier = pltpu.get_barrier_semaphore()

    def there(device):
        return (device >= 0) & (device < count)

    for d in OFFSETS:

        @pl.when(there(me + d))
        def _(d=d):
            pl.semaphore_signal(
                barrier, inc=1, device_id={"cell": me + d}, device_id_type=pl.DeviceIdType.MESH
            )

    @pl.loop(0, feats.shape[0])
    def _(g):
        shell[g, :64] = feats[g, :64]
        shell[g, 64:128] = feats[g, 448:]
        wide[...] = feats[g].astype(jnp.float32)
        for a in range(1, 7):
            start = 128 + (a - 1) * 32
            lines = [
                wide[a * 64 : a * 64 + 8],
                wide[a * 64 + 56 : a * 64 + 64],
                wide[pl.ds(a * 64, 8, stride=8)],
                wide[pl.ds(a * 64 + 7, 8, stride=8)],
            ]
            shell[g, start : start + 32] = jnp.concatenate(lines).astype(jnp.bfloat16)

    for i, out in enumerate((out0, out1, out2, out3)):
        for slot in range(out.shape[0]):
            out[slot] = shell[lists[i, slot]]

    pl.semaphore_wait(barrier, sum(there(me + d).astype(jnp.int32) for d in OFFSETS))

    copies = []
    for i, (d, out, into) in enumerate(
        zip(OFFSETS, (out0, out1, out2, out3), (in0, in1, in2, in3))
    ):
        copy = pltpu.make_async_remote_copy(
            src_ref=out,
            dst_ref=into,
            send_sem=sent.at[i],
            recv_sem=landed.at[i],
            device_id={"cell": me + d},
            device_id_type=pl.DeviceIdType.MESH,
        )
        copies.append(copy)
        pl.when(there(me + d))(copy.start)
    for d, into, copy in zip(OFFSETS, (in0, in1, in2, in3), copies):

        @pl.when(there(me - d))
        def _(copy=copy):
            copy.wait_recv()

        @pl.when(jnp.logical_not(there(me - d)))
        def _(into=into):
            into[...] = jnp.zeros_like(into)

        @pl.when(there(me + d))
        def _(copy=copy):
            copy.wait_send()


def fill_columns(g, ids, own, ext, cols):
    z = lax.broadcasted_iota(jnp.int32, (8, 8, 128), 1)

    def rows_of(number, start, size):
        return ext[ids[g, number - (number > 13)], start : start + size].astype(jnp.float32)

    def spread(line):
        return jnp.broadcast_to(line[:, None, :], (8, 8, 128))

    def shifts(low, mid, high):
        mask = z[: mid.shape[0]]
        return (
            pltpu.roll(jnp.where(mask == 7, low, mid), 1, 1),
            mid,
            pltpu.roll(jnp.where(mask == 0, high, mid), 7, 1),
        )

    def store(place, bands):
        for kz in range(3):
            whole = jnp.concatenate([bands[0][kz], bands[1][kz], bands[2][kz]], axis=0)
            for ky in range(3):
                column = 3 * ky + kz
                cols[place, :, column * 128 : (column + 1) * 128] = (
                    whole[ky : ky + 8].reshape(64, 128).astype(jnp.bfloat16)
                )

    def end_plane(place, ox, start):
        bands = []
        for oy in (-1, 0, 1):
            first = 9 * (ox + 1) + 3 * (oy + 1)
            low, size = {-1: (48, 16), 0: (0, 64), 1: (0, 16)}[oy]
            parts = []
            for i in range(3):
                part = rows_of(first + i, start + low, size).reshape(size // 8, 8, 128)
                parts.append({-1: part[1:], 0: part, 1: part[:1]}[oy])
            bands.append(shifts(*parts))
        store(place, bands)

    def inner_plane(a):
        def line(number, which):
            if a in (0, 7):
                start = 0 if a == 0 else 64
                if which < 2:
                    return rows_of(number, start + 48 * which, 16)[8 * which : 8 * which + 8]
                return rows_of(number, start, 64).reshape(8, 8, 128)
            rows = rows_of(number, 128 + (a - 1) * 32 + 16 * (which // 2), 16)
            return rows[8 * (which % 2) : 8 * (which % 2) + 8]

        mid = own[g, a * 64 : (a + 1) * 64].astype(jnp.float32).reshape(8, 8, 128)
        sides = [line(12, 3), line(14, 2)]
        if a not in (0, 7):
            sides = [spread(side) for side in sides]
        store(
            a + 1,
            [
                shifts(*(line(9 + i, 1)[None] for i in range(3))),
                shifts(sides[0], mid, sides[1]),
                shifts(*(line(15 + i, 0)[None] for i in range(3))),
            ],
        )

    end_plane(0, -1, 64)
    for a in range(8):
        inner_plane(a)
    end_plane(9, 1, 0)


def conv_kernel(
    ids, own, feats, from0, from1, from2, from3, weight, gain, shift, reduce, order,
    fine, octant, ext, cols, grouped, sems,
):
    g = pl.program_id(0)
    blocks, slots = feats.shape[0], from0.shape[0]

    @pl.when(g == 0)
    def _():
        copies = [pltpu.make_async_copy(feats, ext.at[pl.ds(0, blocks)], sems.at[0])]
        for i, part in enumerate((from0, from1, from2, from3)):
            copies.append(
                pltpu.make_async_copy(
                    part, ext.at[pl.ds(blocks + i * slots, slots)], sems.at[i + 1]
                )
            )
        for copy in copies:
            copy.start()
        ext[blocks + 4 * slots] = jnp.zeros(ext.shape[1:], ext.dtype)
        for copy in copies:
            copy.wait()

    fill_columns(g, ids, own, ext, cols)
    total = None
    for kx in range(3):
        term = jnp.dot(
            cols[kx : kx + 8].reshape(512, 1152),
            weight[kx * 1152 : (kx + 1) * 1152],
            preferred_element_type=jnp.float32,
        )
        total = term if total is None else total + term
    out = jnp.maximum(total * gain[...] + shift[...], 0.0).astype(jnp.bfloat16)
    fine[0] = out
    for a in range(4):
        rows = jnp.dot(
            order[...], out[a * 128 : (a + 1) * 128], preferred_element_type=jnp.float32
        ).astype(jnp.bfloat16)
        for p in range(8):
            grouped[g, a * 16 : (a + 1) * 16, p * 128 : (p + 1) * 128] = rows[p * 16 : (p + 1) * 16]

    @pl.when(g == blocks - 1)
    def _():
        octant[...] = (
            jnp.dot(
                grouped[...].reshape(blocks * 64, 1024),
                reduce[...],
                preferred_element_type=jnp.float32,
            )
            .astype(jnp.bfloat16)
            .reshape(octant.shape)
        )


def place_kernel(targets, mine, other, order, coarse, rows, stack, source):
    count, octants = mine.shape[0], 8 * coarse.shape[0]
    me = lax.axis_index("cell")
    for i in range(octants):
        source[i] = 2 * count
    for part, device in enumerate((me, me + 1 - 2 * (me % 2))):
        for i in range(count):
            place = targets[device * count + i] - (me % 2) * octants

            @pl.when((place >= 0) & (place < octants))
            def _(place=place, row=part * count + i):
                source[place] = row

    rows[:count] = mine[...]
    rows[count : 2 * count] = other[...]
    rows[2 * count] = jnp.zeros(rows.shape[1:], rows.dtype)
    for slot in range(coarse.shape[0]):
        for qx in range(2):
            for a in range(4):
                for q in range(4):
                    stack[q * 16 : (q + 1) * 16] = rows[
                        source[slot * 8 + qx * 4 + q], a * 16 : (a + 1) * 16
                    ]
                start = (4 * qx + a) * 64
                coarse[slot, start : start + 64] = jnp.dot(
                    order[...], stack[...], preferred_element_type=jnp.float32
                ).astype(jnp.bfloat16)


def per_device(
    features,
    neighbour_table,
    send_lists,
    coarse_target,
    conv_weight,
    norm_gain,
    norm_shift,
    reduce_weight_matrix,
):
    blocks = features.shape[0]
    slots = send_lists.shape[2]
    channels = features.shape[2]
    vmem = pl.BlockSpec(memory_space=pltpu.VMEM)
    smem = pl.BlockSpec(memory_space=pltpu.SMEM)
    hbm = pl.BlockSpec(memory_space=pl.ANY)
    rows = 320
    shell, *received = pl.pallas_call(
        exchange_kernel,
        in_specs=[smem, vmem],
        out_specs=[vmem] * 5,
        out_shape=[jax.ShapeDtypeStruct((blocks, rows, channels), jnp.bfloat16)]
        + [jax.ShapeDtypeStruct((slots, rows, channels), jnp.bfloat16)] * 4,
        scratch_shapes=[pltpu.VMEM((512, channels), jnp.float32)]
        + [pltpu.VMEM((slots, rows, channels), jnp.bfloat16)] * 4
        + [pltpu.SemaphoreType.DMA((4,)), pltpu.SemaphoreType.DMA((4,))],
        compiler_params=pltpu.CompilerParams(
            vmem_limit_bytes=24 * 1024 * 1024, collective_id=0, has_side_effects=True
        ),
    )(send_lists[0], features)
    fine, octants = pl.pallas_call(
        conv_kernel,
        grid_spec=pltpu.PrefetchScalarGridSpec(
            num_scalar_prefetch=1,
            grid=(blocks,),
            in_specs=[vmem] + [hbm] * 5 + [vmem] * 5,
            out_specs=[
                pl.BlockSpec((1, 512, channels), lambda g, ids: (g, 0, 0)),
                pl.BlockSpec((blocks, 64, channels), lambda g, ids: (0, 0, 0)),
            ],
            scratch_shapes=[
                pltpu.VMEM((blocks + 4 * slots + 1, rows, channels), jnp.bfloat16),
                pltpu.VMEM((10, 64, 9 * channels), jnp.bfloat16),
                pltpu.VMEM((blocks, 64, 8 * channels), jnp.bfloat16),
                pltpu.SemaphoreType.DMA((5,)),
            ],
        ),
        out_shape=[
            jax.ShapeDtypeStruct((blocks, 512, channels), jnp.bfloat16),
            jax.ShapeDtypeStruct((blocks, 64, channels), jnp.bfloat16),
        ],
        compiler_params=pltpu.CompilerParams(vmem_limit_bytes=40 * 1024 * 1024),
    )(
        neighbour_table, features, shell, *received, conv_weight, norm_gain[None], norm_shift[None],
        reduce_weight_matrix, octant_order(),
    )
    partner_octants = swapped(octants, "cell")
    coarse_slots = blocks // 4
    coarse = pl.pallas_call(
        place_kernel,
        in_specs=[smem, vmem, vmem, vmem],
        out_specs=vmem,
        out_shape=jax.ShapeDtypeStruct((coarse_slots, 512, channels), jnp.bfloat16),
        scratch_shapes=[
            pltpu.VMEM((2 * blocks + 1, 64, channels), jnp.bfloat16),
            pltpu.VMEM((64, channels), jnp.bfloat16),
            pltpu.SMEM((8 * coarse_slots,), jnp.int32),
        ],
        compiler_params=pltpu.CompilerParams(vmem_limit_bytes=16 * 1024 * 1024),
    )(coarse_target, octants, partner_octants, coarse_order())
    return (fine, coarse)


def solution(mesh):
    return jax.shard_map(
        per_device,
        mesh=mesh,
        in_specs=(
            P(("groups", "cell"), None, None),
            P(("groups", "cell"), None),
            P(("groups", "cell"), None, None),
            P("groups"),
            P(),
            P(),
            P(),
            P(),
        ),
        out_specs=(P(("groups", "cell"), None, None), P(("groups", "cell"), None, None)),
        check_vma=False,
    )
```

```python
import jax
import jax.numpy as jnp
import numpy as np
from jax import lax
from jax.experimental import pallas as pl
from jax.experimental.pallas import tpu as pltpu
from jax.sharding import PartitionSpec as P

OFFSETS = (1, -1, 2, -2)


def swapped(block, axis):
    count = lax.axis_size(axis)
    return lax.ppermute(block, axis, [(i, i ^ 1) for i in range(count)])


def octant_order():
    r = lax.broadcasted_iota(jnp.int32, (128, 128), 0)
    column = lax.broadcasted_iota(jnp.int32, (128, 128), 1)
    px, py, pz = r >> 6, (r >> 5) & 1, (r >> 4) & 1
    b, c = (r >> 2) & 3, r & 3
    hit = column == px * 64 + (2 * b + py) * 8 + 2 * c + pz
    return jnp.where(hit, 1.0, 0.0).astype(jnp.bfloat16)


def coarse_order():
    order = np.zeros((64, 64), np.float32)
    for q in range(4):
        qy, qz = q // 2, q % 2
        for b in range(4):
            for c in range(4):
                order[(4 * qy + b) * 8 + 4 * qz + c, q * 16 + b * 4 + c] = 1
    return jnp.asarray(order, jnp.bfloat16)


def exchange_kernel(
    lists, feats, shell, in0, in1, in2, in3, wide, out0, out1, out2, out3, sent, landed
):
    me, count = lax.axis_index("cell"), lax.axis_size("cell")
    barrier = pltpu.get_barrier_semaphore()

    def there(device):
        return (device >= 0) & (device < count)

    for d in OFFSETS:

        @pl.when(there(me + d))
        def _(d=d):
            pl.semaphore_signal(
                barrier, inc=1, device_id={"cell": me + d}, device_id_type=pl.DeviceIdType.MESH
            )

    @pl.loop(0, feats.shape[0])
    def _(g):
        shell[g, :64] = feats[g, :64]
        shell[g, 64:128] = feats[g, 448:]
        wide[...] = feats[g].astype(jnp.float32)
        for a in range(1, 7):
            start = 128 + (a - 1) * 32
            lines = [
                wide[a * 64 : a * 64 + 8],
                wide[a * 64 + 56 : a * 64 + 64],
                wide[pl.ds(a * 64, 8, stride=8)],
                wide[pl.ds(a * 64 + 7, 8, stride=8)],
            ]
            shell[g, start : start + 32] = jnp.concatenate(lines).astype(jnp.bfloat16)

    for i, out in enumerate((out0, out1, out2, out3)):
        for slot in range(out.shape[0]):
            out[slot] = shell[lists[i, slot]]

    pl.semaphore_wait(barrier, sum(there(me + d).astype(jnp.int32) for d in OFFSETS))

    copies = []
    for i, (d, out, into) in enumerate(
        zip(OFFSETS, (out0, out1, out2, out3), (in0, in1, in2, in3))
    ):
        copy = pltpu.make_async_remote_copy(
            src_ref=out,
            dst_ref=into,
            send_sem=sent.at[i],
            recv_sem=landed.at[i],
            device_id={"cell": me + d},
            device_id_type=pl.DeviceIdType.MESH,
        )
        copies.append(copy)
        pl.when(there(me + d))(copy.start)
    for d, into, copy in zip(OFFSETS, (in0, in1, in2, in3), copies):

        @pl.when(there(me - d))
        def _(copy=copy):
            copy.wait_recv()

        @pl.when(jnp.logical_not(there(me - d)))
        def _(into=into):
            into[...] = jnp.zeros_like(into)

        @pl.when(there(me + d))
        def _(copy=copy):
            copy.wait_send()


def fill_columns(g, ids, own, ext, cols):
    z = lax.broadcasted_iota(jnp.int32, (8, 8, 128), 1)

    def rows_of(number, start, size):
        return ext[ids[g, number - (number > 13)], start : start + size].astype(jnp.float32)

    def spread(line):
        return jnp.broadcast_to(line[:, None, :], (8, 8, 128))

    def shifts(low, mid, high):
        mask = z[: mid.shape[0]]
        return (
            pltpu.roll(jnp.where(mask == 7, low, mid), 1, 1),
            mid,
            pltpu.roll(jnp.where(mask == 0, high, mid), 7, 1),
        )

    def store(place, bands):
        for kz in range(3):
            whole = jnp.concatenate([bands[0][kz], bands[1][kz], bands[2][kz]], axis=0)
            for ky in range(3):
                column = 3 * ky + kz
                cols[place, :, column * 128 : (column + 1) * 128] = (
                    whole[ky : ky + 8].reshape(64, 128).astype(jnp.bfloat16)
                )

    def end_plane(place, ox, start):
        bands = []
        for oy in (-1, 0, 1):
            first = 9 * (ox + 1) + 3 * (oy + 1)
            low, size = {-1: (48, 16), 0: (0, 64), 1: (0, 16)}[oy]
            parts = []
            for i in range(3):
                part = rows_of(first + i, start + low, size).reshape(size // 8, 8, 128)
                parts.append({-1: part[1:], 0: part, 1: part[:1]}[oy])
            bands.append(shifts(*parts))
        store(place, bands)

    def inner_plane(a):
        def line(number, which):
            if a in (0, 7):
                start = 0 if a == 0 else 64
                if which < 2:
                    return rows_of(number, start + 48 * which, 16)[8 * which : 8 * which + 8]
                return rows_of(number, start, 64).reshape(8, 8, 128)
            rows = rows_of(number, 128 + (a - 1) * 32 + 16 * (which // 2), 16)
            return rows[8 * (which % 2) : 8 * (which % 2) + 8]

        mid = own[g, a * 64 : (a + 1) * 64].astype(jnp.float32).reshape(8, 8, 128)
        sides = [line(12, 3), line(14, 2)]
        if a not in (0, 7):
            sides = [spread(side) for side in sides]
        store(
            a + 1,
            [
                shifts(*(line(9 + i, 1)[None] for i in range(3))),
                shifts(sides[0], mid, sides[1]),
                shifts(*(line(15 + i, 0)[None] for i in range(3))),
            ],
        )

    end_plane(0, -1, 64)
    for a in range(8):
        inner_plane(a)
    end_plane(9, 1, 0)


def conv_kernel(
    ids, own, feats, from0, from1, from2, from3, weight, gain, shift, reduce,
    fine, octant, ext, cols, grouped, order, sems,
):
    g = pl.program_id(0)
    blocks, slots = feats.shape[0], from0.shape[0]

    @pl.when(g == 0)
    def _():
        copies = [pltpu.make_async_copy(feats, ext.at[pl.ds(0, blocks)], sems.at[0])]
        for i, part in enumerate((from0, from1, from2, from3)):
            copies.append(
                pltpu.make_async_copy(
                    part, ext.at[pl.ds(blocks + i * slots, slots)], sems.at[i + 1]
                )
            )
        for copy in copies:
            copy.start()
        order[...] = octant_order()
        ext[blocks + 4 * slots] = jnp.zeros(ext.shape[1:], ext.dtype)
        for copy in copies:
            copy.wait()

    fill_columns(g, ids, own, ext, cols)
    total = None
    for kx in range(3):
        term = jnp.dot(
            cols[kx : kx + 8].reshape(512, 1152),
            weight[kx * 1152 : (kx + 1) * 1152],
            preferred_element_type=jnp.float32,
        )
        total = term if total is None else total + term
    out = jnp.maximum(total * gain[...] + shift[...], 0.0).astype(jnp.bfloat16)
    fine[0] = out
    for a in range(4):
        rows = jnp.dot(
            order[...], out[a * 128 : (a + 1) * 128], preferred_element_type=jnp.float32
        ).astype(jnp.bfloat16)
        for p in range(8):
            grouped[g, a * 16 : (a + 1) * 16, p * 128 : (p + 1) * 128] = rows[p * 16 : (p + 1) * 16]

    @pl.when(g == blocks - 1)
    def _():
        octant[...] = (
            jnp.dot(
                grouped[...].reshape(blocks * 64, 1024),
                reduce[...],
                preferred_element_type=jnp.float32,
            )
            .astype(jnp.bfloat16)
            .reshape(octant.shape)
        )


def place_kernel(targets, mine, other, order, coarse, rows, stack, source):
    count, octants = mine.shape[0], 8 * coarse.shape[0]
    me = lax.axis_index("cell")
    for i in range(octants):
        source[i] = 2 * count
    for part, device in enumerate((me, me + 1 - 2 * (me % 2))):
        for i in range(count):
            place = targets[device * count + i] - (me % 2) * octants

            @pl.when((place >= 0) & (place < octants))
            def _(place=place, row=part * count + i):
                source[place] = row

    rows[:count] = mine[...]
    rows[count : 2 * count] = other[...]
    rows[2 * count] = jnp.zeros(rows.shape[1:], rows.dtype)
    for slot in range(coarse.shape[0]):
        for qx in range(2):
            for a in range(4):
                for q in range(4):
                    stack[q * 16 : (q + 1) * 16] = rows[
                        source[slot * 8 + qx * 4 + q], a * 16 : (a + 1) * 16
                    ]
                start = (4 * qx + a) * 64
                coarse[slot, start : start + 64] = jnp.dot(
                    order[...], stack[...], preferred_element_type=jnp.float32
                ).astype(jnp.bfloat16)


def per_device(
    features,
    neighbour_table,
    send_lists,
    coarse_target,
    conv_weight,
    norm_gain,
    norm_shift,
    reduce_weight_matrix,
):
    blocks = features.shape[0]
    slots = send_lists.shape[2]
    channels = features.shape[2]
    vmem = pl.BlockSpec(memory_space=pltpu.VMEM)
    smem = pl.BlockSpec(memory_space=pltpu.SMEM)
    hbm = pl.BlockSpec(memory_space=pl.ANY)
    rows = 320
    shell, *received = pl.pallas_call(
        exchange_kernel,
        in_specs=[smem, vmem],
        out_specs=[vmem] * 5,
        out_shape=[jax.ShapeDtypeStruct((blocks, rows, channels), jnp.bfloat16)]
        + [jax.ShapeDtypeStruct((slots, rows, channels), jnp.bfloat16)] * 4,
        scratch_shapes=[pltpu.VMEM((512, channels), jnp.float32)]
        + [pltpu.VMEM((slots, rows, channels), jnp.bfloat16)] * 4
        + [pltpu.SemaphoreType.DMA((4,)), pltpu.SemaphoreType.DMA((4,))],
        compiler_params=pltpu.CompilerParams(
            vmem_limit_bytes=24 * 1024 * 1024, collective_id=0, has_side_effects=True
        ),
    )(send_lists[0], features)
    fine, octants = pl.pallas_call(
        conv_kernel,
        grid_spec=pltpu.PrefetchScalarGridSpec(
            num_scalar_prefetch=1,
            grid=(blocks,),
            in_specs=[vmem] + [hbm] * 5 + [vmem] * 4,
            out_specs=[
                pl.BlockSpec((1, 512, channels), lambda g, ids: (g, 0, 0)),
                pl.BlockSpec((blocks, 64, channels), lambda g, ids: (0, 0, 0)),
            ],
            scratch_shapes=[
                pltpu.VMEM((blocks + 4 * slots + 1, rows, channels), jnp.bfloat16),
                pltpu.VMEM((10, 64, 9 * channels), jnp.bfloat16),
                pltpu.VMEM((blocks, 64, 8 * channels), jnp.bfloat16),
                pltpu.VMEM((128, 128), jnp.bfloat16),
                pltpu.SemaphoreType.DMA((5,)),
            ],
        ),
        out_shape=[
            jax.ShapeDtypeStruct((blocks, 512, channels), jnp.bfloat16),
            jax.ShapeDtypeStruct((blocks, 64, channels), jnp.bfloat16),
        ],
        compiler_params=pltpu.CompilerParams(vmem_limit_bytes=40 * 1024 * 1024),
    )(
        neighbour_table, features, shell, *received, conv_weight, norm_gain[None], norm_shift[None],
        reduce_weight_matrix,
    )
    partner_octants = swapped(octants, "cell")
    coarse_slots = blocks // 4
    coarse = pl.pallas_call(
        place_kernel,
        in_specs=[smem, vmem, vmem, vmem],
        out_specs=vmem,
        out_shape=jax.ShapeDtypeStruct((coarse_slots, 512, channels), jnp.bfloat16),
        scratch_shapes=[
            pltpu.VMEM((2 * blocks + 1, 64, channels), jnp.bfloat16),
            pltpu.VMEM((64, channels), jnp.bfloat16),
            pltpu.SMEM((8 * coarse_slots,), jnp.int32),
        ],
        compiler_params=pltpu.CompilerParams(vmem_limit_bytes=16 * 1024 * 1024),
    )(coarse_target, octants, partner_octants, coarse_order())
    return (fine, coarse)


def solution(mesh):
    return jax.shard_map(
        per_device,
        mesh=mesh,
        in_specs=(
            P(("groups", "cell"), None, None),
            P(("groups", "cell"), None),
            P(("groups", "cell"), None, None),
            P("groups"),
            P(),
            P(),
            P(),
            P(),
        ),
        out_specs=(P(("groups", "cell"), None, None), P(("groups", "cell"), None, None)),
        check_vma=False,
    )
```
